32 devices in a mesh: groups: 2 (over y), ctx: 4 (over z), inner: 2 (over x), chan: 2 (over core).
Axes of the slice: x: 2, y: 2, z: 4, core: 2. Of those that a mesh axis runs over, the one named last changes fastest.
Arguments:
- queries: bfloat16 [2048, 8192], P(('groups', 'ctx', 'inner'), 'chan'), parts along dimension 0, may hold values from -6 to 6
- keys_in: bfloat16 [2048, 8192], P(('groups', 'ctx', 'inner'), 'chan'), parts along dimension 0, may hold values from -6 to 6
- values_in: bfloat16 [2048, 8192], P(('groups', 'ctx', 'inner'), 'chan'), parts along dimension 0, may hold values from -6 to 6
- out_grad: bfloat16 [2048, 8192], P(('groups', 'ctx', 'inner'), 'chan'), parts along dimension 0, may hold values from -6 to 6
- short_taps: float32 [3, 7, 8192], P(None, None, 'chan'), may hold values from -2 to 2
- pole_rate: float32 [16, 512], P(None, 'chan'), may hold values from 0.0001953125 to 0.15, as said below
- residue: float32 [16, 512], P(None, 'chan'), may hold values from -0.55 to 0.55
Outputs:
- query_grad: bfloat16 [2048, 8192], P(('groups', 'ctx', 'inner'), 'chan'), parts along dimension 0
- key_grad: bfloat16 [2048, 8192], P(('groups', 'ctx', 'inner'), 'chan'), parts along dimension 0
- value_grad: bfloat16 [2048, 8192], P(('groups', 'ctx', 'inner'), 'chan'), parts along dimension 0
- tap_grad: float32 [6, 7, 8192], P('groups', None, 'chan'), parts along dimension 0
- rate_grad: float32 [32, 512], P('groups', 'chan'), parts along dimension 0
- residue_grad: float32 [32, 512], P('groups', 'chan'), parts along dimension 0
The draws below stay inside these ranges and needn't reach their ends.
There are 2 independent parts, one for each index of `groups`. The reference program is written for one: setup_inputs(seed, part) draws one part's arguments, and reference() takes and returns one part's arrays. A program takes and returns all parts, laid end to end along the dimension named above; an argument that names none is the same for every part. Nothing has to cross between parts.
Inputs may be any that keep to these rules, and one draw needn't show every extreme that they name: `pole_rate`: each rate lies between 0.2 / 1024 and 0.15.
All inputs are finite; a program needn't handle non-finite values.
Results may differ from the reference program's by a relative error of at most 0.001.
Values may be sent and summed in bfloat16 or wider, within the bound.
A program may use at most 192 MiB of HBM per device.

```python
import jax
import jax.numpy as jnp
from jax import lax

D = 8192
ORDER = 16
KSIZE = 7
GS = 16
ROWS = 128
GROUPS = 512
TOKENS = 1024


def modal_pair(key):
    base_key = jax.random.fold_in(key, 4242)
    pick_key, slow_key, middle_key, fast_key, sign_key = jax.random.split(base_key, 5)
    slow_share = 0.35
    middle_share = 0.3
    picker = jax.random.uniform(pick_key, (ORDER, GROUPS))
    slow_mask = picker < slow_share
    middle_mask = picker < slow_share + middle_share
    slow_rate = jnp.exp(jax.random.uniform(slow_key, (ORDER, GROUPS), minval=jnp.log(0.2 / TOKENS), maxval=jnp.log(2.0 / TOKENS)))
    middle_rate = jnp.exp(jax.random.uniform(middle_key, (ORDER, GROUPS), minval=jnp.log(0.002), maxval=jnp.log(0.06)))
    fast_rate = jnp.exp(jax.random.uniform(fast_key, (ORDER, GROUPS), minval=jnp.log(0.06), maxval=jnp.log(0.15)))
    rate_table = jnp.where(slow_mask, slow_rate, jnp.where(middle_mask, middle_rate, fast_rate)).astype(jnp.float32)
    amplitude = jnp.clip(jax.random.normal(sign_key, (ORDER, GROUPS)), -4.0, 4.0)
    return (rate_table, (amplitude * jnp.sqrt(2.0 * rate_table) * 0.25).astype(jnp.float32))


def draw_pole_rate(key, part):
    return modal_pair(key)[0]


def draw_residue(key, part):
    return modal_pair(key)[1]


def level_of(key, dims, cuts, low, largest):
    def one(dim, shards_of):
        heights = jax.random.uniform(jax.random.fold_in(jax.random.fold_in(key, 6), dim), (shards_of,), jnp.float32, low / len(cuts), largest / len(cuts))
        return jnp.repeat(jnp.exp(heights), dims[dim] // shards_of).reshape((-1,) + (1,) * (len(dims) - dim - 1))

    level = one(*cuts[0])
    for cut in cuts[1:]:
        level = level * one(*cut)
    return level


def scatter_about(rng, shape, width, most, cuts=(), kind=jnp.bfloat16):
    array = jax.random.normal(rng, shape, jnp.float32) * width
    if len(cuts) > 0:
        array = level_of(rng, shape, cuts, -0.22, 0.18) * array
    return jnp.clip(array, min=-most, max=most).astype(kind)


def setup_inputs(seed: int = 0, part: int = 0) -> dict:
    arg_keys = jax.random.split(jax.random.key(seed), 8)
    own_keys = jax.random.split(jax.random.fold_in(arg_keys[7], part), 8)
    queries = scatter_about(own_keys[0], (TOKENS, D), 1.0, 6.0, ((0, 8), (1, 2)))
    keys_in = scatter_about(own_keys[1], (TOKENS, D), 1.0, 6.0, ((0, 8), (1, 2)))
    values_in = scatter_about(own_keys[2], (TOKENS, D), 1.0, 6.0, ((0, 8), (1, 2)))
    out_grad = scatter_about(own_keys[3], (TOKENS, D), 1.0, 6.0, ((0, 8), (1, 2)))
    short_taps = scatter_about(arg_keys[4], (3, KSIZE, D), KSIZE ** -0.5, 2.0, ((2, 2),), jnp.float32)
    pole_rate = draw_pole_rate(jax.random.fold_in(arg_keys[7], 71), part)
    residue = draw_residue(jax.random.fold_in(arg_keys[7], 71), part)
    return {"queries": queries, "keys_in": keys_in, "values_in": values_in, "out_grad": out_grad, "short_taps": short_taps, "pole_rate": pole_rate, "residue": residue}


def causal_conv(signal, taps):
    tap_count = taps.shape[0]
    length = signal.shape[0]
    padded = jnp.concatenate([jnp.zeros((tap_count - 1, signal.shape[1]), signal.dtype), signal], axis=0)
    running = jnp.zeros_like(signal)
    for lag_index in range(tap_count):
        offset_row = tap_count - 1 - lag_index
        running = running + taps[lag_index] * padded[offset_row:offset_row + length]
    return running

def mixer(queries, keys_in, values_in, short_taps, pole_rate, residue):
    query_mix = causal_conv(queries, short_taps[0])
    key_mix = causal_conv(keys_in, short_taps[1])
    value_mix = causal_conv(values_in, short_taps[2])
    source_term = key_mix * value_mix
    decay_rows = jnp.repeat(jnp.exp(-pole_rate), GS, axis=1)
    residue_rows = jnp.repeat(residue, GS, axis=1)
    blocks = source_term.reshape(TOKENS // ROWS, ROWS, D)

    def one_step(inner_state, source_row):
        new_state = decay_rows * inner_state + source_row[None, :]
        return (new_state, lax.optimization_barrier(jnp.sum(residue_rows * new_state, axis=0)))

    def block_body(outer_state, source_block):
        return lax.scan(one_step, outer_state, source_block)
    final_state, long_out = lax.scan(jax.checkpoint(block_body), jnp.zeros((ORDER, D), jnp.float32), blocks)
    return query_mix * long_out.reshape(TOKENS, D)

def reference(queries, keys_in, values_in, out_grad, short_taps, pole_rate, residue):
    result, pullback = jax.vjp(mixer, queries.astype(jnp.float32), keys_in.astype(jnp.float32), values_in.astype(jnp.float32), short_taps, pole_rate, residue)
    grads = pullback(out_grad.astype(jnp.float32))
    query_grad = grads[0].astype(jnp.bfloat16)
    key_grad = grads[1].astype(jnp.bfloat16)
    value_grad = grads[2].astype(jnp.bfloat16)
    tap_grad = grads[3] / jnp.sqrt(jnp.float32(TOKENS))
    rate_grad = grads[4] / jnp.float32(TOKENS)
    residue_grad = grads[5] / jnp.float32(TOKENS)
    return (query_grad, key_grad, value_grad, tap_grad, rate_grad, residue_grad)
```

```python
import functools

import jax
import jax.numpy as jnp
from jax import lax
from jax.experimental import pallas as pl
from jax.experimental.pallas import tpu as pltpu
from jax.sharding import PartitionSpec as P

LINE = ("ctx", "inner")
LANES = 128
SUB = 8
EXACT = lax.Precision.HIGHEST


def moved(block, distance):
    devices = range(lax.axis_size(LINE))
    return lax.ppermute(block, LINE, [(i, i + distance) for i in devices if i + distance in devices])


def carried_in(total, decay, reverse):
    sign = -1 if reverse else 1
    count = lax.axis_size(LINE)
    state = moved(total, sign)
    distance = 1
    while distance < count - 1:
        state = state + decay * moved(state, sign * distance)
        decay = decay * decay
        distance *= 2
    return state


def summed(block):
    count = lax.axis_size(LINE)
    distance = 1
    while distance < count:
        block = block + lax.ppermute(block, LINE, [(i, i ^ distance) for i in range(count)])
        distance *= 2
    return block


def spread_matrix(local_groups, width, members):
    first = pl.program_id(0) * width
    row = lax.broadcasted_iota(jnp.int32, (local_groups, width), 0)
    col = lax.broadcasted_iota(jnp.int32, (local_groups, width), 1) + first
    low = row * members
    return jnp.where((col >= low) & (col < low + members), 1.0, 0.0).astype(jnp.float32)


def first_kernel(members, q_ref, k_ref, v_ref, g_ref, prev_ref, next_ref, taps_ref, rate_ref, res_ref,
                 mix_ref, ef_ref, ea_ref, final_ref, first_ref, rates_ref, ress_ref, wide, src, adj, each):
    rows, width = q_ref.shape
    modes, local_groups = rate_ref.shape
    tap_count = taps_ref.shape[1]
    steps = rows // SUB
    onto = spread_matrix(local_groups, width, members)
    rates_ref[...] = jnp.dot(rate_ref[...], onto, precision=EXACT, preferred_element_type=jnp.float32)
    ress_ref[...] = jnp.dot(res_ref[...], onto, precision=EXACT, preferred_element_type=jnp.float32)
    for i, x_ref in enumerate((q_ref, k_ref, v_ref)):
        wide[i, 0:SUB] = prev_ref[i]
        wide[i, SUB:SUB + rows] = x_ref[...].astype(jnp.float32)
        wide[i, SUB + rows:] = next_ref[i]
    chunk = lax.broadcasted_iota(jnp.int32, (SUB, LANES), 0).astype(jnp.float32)

    @pl.loop(0, width // LANES)
    def _(column):
        cols = pl.ds(pl.multiple_of(column * LANES, LANES), LANES)
        mixes = []
        for i in range(3):
            total = taps_ref[i, 0:1, cols] * wide[i, SUB:, cols]
            for j in range(1, tap_count):
                total = total + taps_ref[i, j:j + 1, cols] * wide[i, SUB - j:2 * SUB + rows - j, cols]
            mix_ref[i, :, cols] = total
            mixes.append(total[:rows])
        src[:, :] = mixes[1] * mixes[2]
        adj[:, :] = mixes[0] * g_ref[:, cols].astype(jnp.float32)
        s = [src[pl.ds(j, SUB, stride=steps), :] for j in range(steps)]
        a = [adj[pl.ds(j, SUB, stride=steps), :] for j in range(steps)]

        for n in range(modes):
            each[0, n] = jnp.broadcast_to(rates_ref[n:n + 1, cols], (SUB, LANES))

        def one(n, nothing):
            rate = each[0, n]
            lam = jnp.exp(-rate)
            ahead = s[0]
            back = a[steps - 1]
            for j in range(1, steps):
                ahead = lam * ahead + s[j]
                back = lam * back + a[steps - 1 - j]
            ef_ref[n, :, cols] = ahead
            ea_ref[n, :, cols] = back
            later = jnp.exp(rate * ((chunk - (SUB - 1)) * float(steps)))
            sooner = jnp.exp(rate * (chunk * -float(steps)))
            each[1, n] = ahead * later
            each[2, n] = back * sooner
            return nothing

        lax.fori_loop(0, modes, one, 0, unroll=4)
        final_ref[:, cols] = jnp.sum(each[1], axis=1)
        first_ref[:, cols] = jnp.sum(each[2], axis=1)


def second_kernel(members, q_ref, k_ref, v_ref, g_ref, prev_ref, gnext_ref, taps_ref, mix_ref, ef_ref, ea_ref,
                  final_ref, rates_ref, ress_ref, sin_ref, pin_ref,
                  qg_ref, kg_ref, vg_ref, tap_ref, mode_ref, pole_ref,
                  wide, src, adj, long_out, long_adj, back, mode_rows, pole_rows, each):
    rows, width = q_ref.shape
    modes = rates_ref.shape[0]
    local_groups = mode_ref.shape[1]
    tap_count = taps_ref.shape[1]
    steps = rows // SUB
    for i, x_ref in enumerate((q_ref, k_ref, v_ref)):
        wide[i, 0:SUB] = prev_ref[i]
        wide[i, SUB:] = x_ref[...].astype(jnp.float32)
    chunk = lax.broadcasted_iota(jnp.int32, (SUB, LANES), 0)

    @pl.loop(0, width // LANES)
    def _(column):
        cols = pl.ds(pl.multiple_of(column * LANES, LANES), LANES)
        src[:, :] = mix_ref[1, :, cols] * mix_ref[2, :, cols]
        adj[:rows, :] = mix_ref[0, :rows, cols] * g_ref[:, cols].astype(jnp.float32)
        adj[rows:, :] = mix_ref[0, rows:, cols] * gnext_ref[:, cols]
        s = [src[pl.ds(j, SUB, stride=steps), :] for j in range(steps)]
        a = [adj[pl.ds(j, SUB, stride=steps), :] for j in range(steps)]
        zero = jnp.zeros((SUB, LANES), jnp.float32)

        lam_table = jnp.exp(-rates_ref[:, cols])
        decay_table = jnp.exp(rates_ref[:, cols] * -float(steps))
        tables = (lam_table, ress_ref[:, cols], decay_table, sin_ref[:, cols], pin_ref[:, cols])
        for i, table in enumerate(tables):
            for n in range(modes):
                each[i, n] = jnp.broadcast_to(table[n:n + 1], (SUB, LANES))

        def one(n, sums):
            outs, adjs = list(sums[0]), list(sums[1])
            lam, res, decay = each[0, n], each[1, n], each[2, n]
            state = jnp.where(chunk == 0, each[3, n], pltpu.roll(ef_ref[n, :, cols], 1, 0))
            late = jnp.where(chunk == SUB - 1, each[4, n], pltpu.roll(ea_ref[n, :, cols], SUB - 1, 0))
            distance = 1
            while distance < SUB:
                state = state + jnp.where(chunk >= distance, decay * pltpu.roll(state, distance, 0), 0.0)
                late = late + jnp.where(chunk < SUB - distance, decay * pltpu.roll(late, SUB - distance, 0), 0.0)
                decay = decay * decay
                distance *= 2
            states = [state]
            mode_sum = zero
            for j in range(steps):
                state = lam * state + s[j]
                states.append(state)
                outs[j] = outs[j] + res * state
                mode_sum = mode_sum + a[j] * state
            pole_sum = zero
            for j in range(steps - 1, -1, -1):
                late = lam * late + a[j]
                adjs[j] = adjs[j] + res * late
                pole_sum = pole_sum + late * states[j]
            each[5, n] = mode_sum
            each[6, n] = lam * res * pole_sum
            return tuple(outs), tuple(adjs)

        outs, adjs = lax.fori_loop(0, modes, one, ((zero,) * steps, (zero,) * steps))
        mode_rows[:, cols] = jnp.sum(each[5], axis=1)
        pole_rows[:, cols] = jnp.sum(each[6], axis=1)
        for j in range(steps):
            long_out[pl.ds(j, SUB, stride=steps), :] = outs[j]
            long_adj[pl.ds(j, SUB, stride=steps), :] = adjs[j]
        rate = rates_ref[:, cols]
        res = ress_ref[:, cols]
        lam = jnp.exp(-rate)
        grow = jnp.exp(rate)
        state = jnp.exp(rate * -float(rows)) * sin_ref[:, cols] + final_ref[:, cols]
        late = pin_ref[:, cols]
        long_out[rows:, :] = zero
        long_adj[rows:, :] = zero
        for j in range(tap_count - 1):
            state = lam * state + src[rows + j:rows + j + 1, :]
            long_out[rows + j:rows + j + 1, :] = jnp.sum(res * state, axis=0, keepdims=True)
            long_adj[rows + j:rows + j + 1, :] = jnp.sum(res * late, axis=0, keepdims=True)
            late = (late - adj[rows + j:rows + j + 1, :]) * grow
        back[0, :rows, cols] = g_ref[:, cols].astype(jnp.float32) * long_out[:rows, :]
        back[0, rows:, cols] = gnext_ref[:, cols] * long_out[rows:, :]
        back[1, :, cols] = long_adj[:, :] * mix_ref[2, :, cols]
        back[2, :, cols] = long_adj[:, :] * mix_ref[1, :, cols]
        for i, grad_ref in enumerate((qg_ref, kg_ref, vg_ref)):
            mine = back[i, 0:rows, cols]
            total = taps_ref[i, 0:1, cols] * mine
            for j in range(1, tap_count):
                total = total + taps_ref[i, j:j + 1, cols] * back[i, j:j + rows, cols]
            grad_ref[:, cols] = total.astype(grad_ref.dtype)
            for j in range(tap_count):
                tap_ref[i, j:j + 1, cols] = jnp.sum(
                    mine * wide[i, SUB - j:SUB - j + rows, cols], axis=0, keepdims=True
                )
            for j in range(tap_count, SUB):
                tap_ref[i, j:j + 1, cols] = jnp.zeros((1, LANES), jnp.float32)

    onto = spread_matrix(local_groups, width, members)
    along = (((1,), (1,)), ((), ()))

    @pl.when(pl.program_id(0) == 0)
    def _():
        mode_ref[...] = jnp.zeros_like(mode_ref)
        pole_ref[...] = jnp.zeros_like(pole_ref)

    mode_ref[...] += lax.dot_general(
        mode_rows[...], onto, along, precision=EXACT, preferred_element_type=jnp.float32
    )
    pole_ref[...] += lax.dot_general(
        pole_rows[...], onto, along, precision=EXACT, preferred_element_type=jnp.float32
    )


def on_device(queries, keys_in, values_in, out_grad, short_taps, pole_rate, residue):
    rows, chans = queries.shape
    modes, local_groups = pole_rate.shape
    members = chans // local_groups
    tap_count = short_taps.shape[1]
    token_total = rows * lax.axis_size(LINE)
    width = min(512, chans)
    f32 = jnp.float32
    tails = jnp.stack([x[rows - SUB:] for x in (queries, keys_in, values_in)])
    heads = jnp.stack([x[:SUB] for x in (queries, keys_in, values_in, out_grad)])
    before = moved(tails, 1).astype(f32)
    after = moved(heads, -1).astype(f32)

    def cut(*lead):
        zeros = (0,) * len(lead)
        return pl.BlockSpec((*lead, width), lambda i: (*zeros, i))

    def full(*shape):
        zeros = (0,) * len(shape)
        return pl.BlockSpec(shape, lambda i: zeros)

    def arr(*shape, dtype=f32):
        return jax.ShapeDtypeStruct(shape, dtype)

    params = pltpu.CompilerParams(vmem_limit_bytes=48 * 1024 * 1024)
    wide_rows = rows + SUB
    streams = [cut(rows)] * 4
    mix, ef, ea, final, first, rates, ress = pl.pallas_call(
        functools.partial(first_kernel, members),
        grid=(chans // width,),
        in_specs=streams + [
            cut(3, SUB), cut(3, SUB), cut(3, tap_count), full(modes, local_groups), full(modes, local_groups)
        ],
        out_specs=[cut(3, wide_rows), cut(modes, SUB), cut(modes, SUB)] + [cut(modes)] * 4,
        out_shape=[arr(3, wide_rows, chans), arr(modes, SUB, chans), arr(modes, SUB, chans)]
        + [arr(modes, chans)] * 4,
        scratch_shapes=[
            pltpu.VMEM((3, wide_rows + SUB, width), f32),
            pltpu.VMEM((rows, LANES), f32),
            pltpu.VMEM((rows, LANES), f32),
            pltpu.VMEM((3, modes, SUB, LANES), f32),
        ],
        compiler_params=params,
        name="local_states",
    )(queries, keys_in, values_in, out_grad, before, after[:3], short_taps, pole_rate, residue)
    decay = jnp.exp(rates * -float(rows))
    state_in = carried_in(final, decay, False)
    late_in = carried_in(first, decay, True)
    query_grad, key_grad, value_grad, taps_sum, mode_sum, pole_sum = pl.pallas_call(
        functools.partial(second_kernel, members),
        grid=(chans // width,),
        in_specs=streams + [
            cut(3, SUB), cut(SUB), cut(3, tap_count), cut(3, wide_rows), cut(modes, SUB), cut(modes, SUB)
        ] + [cut(modes)] * 5,
        out_specs=[cut(rows)] * 3 + [cut(3, SUB), full(modes, local_groups), full(modes, local_groups)],
        out_shape=[arr(rows, chans, dtype=jnp.bfloat16)] * 3
        + [arr(3, SUB, chans), arr(modes, local_groups), arr(modes, local_groups)],
        scratch_shapes=[pltpu.VMEM((3, wide_rows, width), f32)]
        + [pltpu.VMEM((wide_rows, LANES), f32)] * 4
        + [pltpu.VMEM((3, wide_rows, width), f32)]
        + [pltpu.VMEM((modes, width), f32)] * 2
        + [pltpu.VMEM((7, modes, SUB, LANES), f32)],
        compiler_params=params,
        name="gradients",
    )(queries, keys_in, values_in, out_grad, before, after[3], short_taps, mix, ef, ea,
      final, rates, ress, state_in, late_in)
    taps_sum, mode_sum, pole_sum = summed_all(taps_sum, mode_sum, pole_sum)
    tap_grad = taps_sum[:, :tap_count] / jnp.sqrt(f32(token_total))
    return (query_grad, key_grad, value_grad, tap_grad, -pole_sum / f32(token_total), mode_sum / f32(token_total))


def summed_all(taps_sum, mode_sum, pole_sum):
    both = summed(jnp.stack([mode_sum, pole_sum]))
    return summed(taps_sum), both[0], both[1]


def solution(mesh):
    tokens = P(("groups", "ctx", "inner"), "chan")
    return jax.shard_map(
        on_device,
        mesh=mesh,
        in_specs=(tokens, tokens, tokens, tokens, P(None, None, "chan"), P(None, "chan"), P(None, "chan")),
        out_specs=(
            tokens,
            tokens,
            tokens,
            P("groups", None, "chan"),
            P("groups", "chan"),
            P("groups", "chan"),
        ),
        check_vma=False,
    )
```

```python
import functools

import jax
import jax.numpy as jnp
from jax import lax
from jax.experimental import pallas as pl
from jax.experimental.pallas import tpu as pltpu
from jax.sharding import PartitionSpec as P

LINE = ("ctx", "inner")
LANES = 128
SUB = 8
TOGETHER = 4
PIECE = 1024
MESH = pl.DeviceIdType.MESH
EXACT = lax.Precision.HIGHEST


def moved(block, distance):
    devices = range(lax.axis_size(LINE))
    return lax.ppermute(block, LINE, [(i, i + distance) for i in devices if i + distance in devices])


def place_of(position):
    inner = lax.axis_size("inner")
    return {"ctx": position // inner, "inner": position % inner}


def carry_kernel(pieces, rows, final_ref, first_ref, rates_ref, sin_ref, pin_ref, near, outward, entering,
                 near_send, near_recv, far_send, far_recv, give_send, give_recv):
    inner, outer = lax.axis_size("inner"), lax.axis_size("ctx")
    x, z = lax.axis_index("inner"), lax.axis_index("ctx")
    width = final_ref.shape[1] // pieces
    barrier = pltpu.get_barrier_semaphore()
    others = [lax.rem(x + d, inner) for d in range(1, inner)]
    for other in others:
        pl.semaphore_signal(barrier, inc=1, device_id={"inner": other}, device_id_type=MESH)

    @pl.when(z > 0)
    def _():
        pl.semaphore_signal(barrier, inc=1, device_id={"ctx": z - 1}, device_id_type=MESH)

    @pl.when(z < outer - 1)
    def _():
        pl.semaphore_signal(barrier, inc=1, device_id={"ctx": z + 1}, device_id_type=MESH)

    pl.semaphore_wait(barrier, inner - 1 + jnp.where(z > 0, 1, 0) + jnp.where(z < outer - 1, 1, 0))

    def copy(source, target, send, recv, where):
        return pltpu.make_async_remote_copy(
            src_ref=source, dst_ref=target, send_sem=send, recv_sem=recv, device_id=where, device_id_type=MESH
        )

    lines = []
    for line, total_ref, into_ref in ((0, final_ref, sin_ref), (1, first_ref, pin_ref)):
        xs, zs = (x, z) if line == 0 else (inner - 1 - x, outer - 1 - z)
        lines.append((line, total_ref, into_ref, xs, zs, 1 if line == 0 else -1))

    def near_copy(line, total_ref, piece, steps, sign):
        cols = pl.ds(piece * width, width)
        return copy(
            total_ref.at[:, cols], near.at[line, steps - 1, :, cols],
            near_send.at[line, steps - 1, piece], near_recv.at[line, steps - 1, piece],
            {"inner": lax.rem(x + sign * steps + inner, inner)},
        )

    def far_copy(line, piece, sign):
        cols = pl.ds(piece * width, width)
        return copy(
            outward.at[line, :, cols], entering.at[line, :, cols],
            far_send.at[line, piece], far_recv.at[line, piece],
            {"ctx": lax.rem(z + sign + outer, outer)},
        )

    def give_copy(line, piece, steps, sign):
        cols = pl.ds(piece * width, width)
        return copy(
            entering.at[line, :, cols], entering.at[line, :, cols],
            give_send.at[line, steps - 1, piece], give_recv.at[line, piece],
            {"inner": lax.rem(x - sign * steps + inner, inner)},
        )

    for piece in range(pieces):
        for line, total_ref, _, xs, _, sign in lines:
            for steps in range(1, inner):
                @pl.when(xs + steps < inner)
                def _():
                    near_copy(line, total_ref, piece, steps, sign).start()

    for piece in range(pieces):
        cols = pl.ds(piece * width, width)
        decay = jnp.exp(rates_ref[:, cols] * -float(rows))
        for line, total_ref, into_ref, xs, zs, sign in lines:
            @pl.when(xs == inner - 1)
            def _():
                total = jnp.zeros_like(into_ref[:, cols])
                for steps in range(inner - 1, 0, -1):
                    near_copy(line, total_ref, piece, steps, sign).wait_recv()
                    total = decay * total + near[line, steps - 1, :, cols]
                into_ref[:, cols] = total

                @pl.when(zs == 0)
                def _():
                    entering[line, :, cols] = jnp.zeros_like(total)

                @pl.when(zs > 0)
                def _():
                    far_copy(line, piece, sign).wait_recv()

                power = jnp.exp(rates_ref[:, cols] * -float(rows * (inner - 1)))
                mine = power * entering[line, :, cols] + into_ref[:, cols]
                into_ref[:, cols] = mine

                @pl.when(zs < outer - 1)
                def _():
                    outward[line, :, cols] = decay * mine + total_ref[:, cols]
                    far_copy(line, piece, sign).start()

                for steps in range(1, inner):
                    give_copy(line, piece, steps, sign).start()

    for piece in range(pieces):
        cols = pl.ds(piece * width, width)
        decay = jnp.exp(rates_ref[:, cols] * -float(rows))
        for line, total_ref, into_ref, xs, zs, sign in lines:
            @pl.when(xs < inner - 1)
            def _():
                into_ref[:, cols] = jnp.zeros_like(into_ref[:, cols])
                for steps in range(inner - 2, 0, -1):
                    @pl.when(xs >= steps)
                    def _():
                        near_copy(line, total_ref, piece, steps, sign).wait_recv()
                        into_ref[:, cols] = decay * into_ref[:, cols] + near[line, steps - 1, :, cols]

                give_copy(line, piece, 1, sign).wait_recv()
                power = jnp.exp(rates_ref[:, cols] * (-float(rows) * xs.astype(jnp.float32)))
                into_ref[:, cols] = power * entering[line, :, cols] + into_ref[:, cols]

    for piece in range(pieces):
        for line, total_ref, _, xs, zs, sign in lines:
            for steps in range(1, inner):
                @pl.when(xs + steps < inner)
                def _():
                    near_copy(line, total_ref, piece, steps, sign).wait_send()

                @pl.when(xs == inner - 1)
                def _():
                    give_copy(line, piece, steps, sign).wait_send()

            @pl.when((xs == inner - 1) & (zs < outer - 1))
            def _():
                far_copy(line, piece, sign).wait_send()


def carried(final, first, rates, rows):
    modes, chans = final.shape
    pieces = max(1, chans // PIECE)
    hops = max(1, lax.axis_size("inner") - 1)
    shape = jax.ShapeDtypeStruct((modes, chans), jnp.float32)
    vmem = pl.BlockSpec(memory_space=pltpu.VMEM)
    return pl.pallas_call(
        functools.partial(carry_kernel, pieces, rows),
        in_specs=[vmem] * 3,
        out_specs=[vmem] * 2,
        out_shape=[shape] * 2,
        scratch_shapes=[
            pltpu.VMEM((2, hops, modes, chans), jnp.float32),
            pltpu.VMEM((2, modes, chans), jnp.float32),
            pltpu.VMEM((2, modes, chans), jnp.float32),
            pltpu.SemaphoreType.DMA((2, hops, pieces)),
            pltpu.SemaphoreType.DMA((2, hops, pieces)),
            pltpu.SemaphoreType.DMA((2, pieces)),
            pltpu.SemaphoreType.DMA((2, pieces)),
            pltpu.SemaphoreType.DMA((2, hops, pieces)),
            pltpu.SemaphoreType.DMA((2, pieces)),
        ],
        compiler_params=pltpu.CompilerParams(
            collective_id=0, has_side_effects=True, vmem_limit_bytes=16 * 1024 * 1024
        ),
        name="carry",
    )(final, first, rates)


def sum_kernel(x_ref, out_ref, land, send_sem, recv_sem):
    count = lax.axis_size(LINE)
    me = lax.axis_index("ctx") * lax.axis_size("inner") + lax.axis_index("inner")
    barrier = pltpu.get_barrier_semaphore()
    others = [lax.rem(me + d, count) for d in range(1, count)]
    for other in others:
        pl.semaphore_signal(barrier, inc=1, device_id=place_of(other), device_id_type=MESH)
    pl.semaphore_wait(barrier, count - 1)

    def copy_of(source, target, phase, d):
        return pltpu.make_async_remote_copy(
            src_ref=source,
            dst_ref=target,
            send_sem=send_sem.at[phase, d],
            recv_sem=recv_sem.at[phase, d],
            device_id=place_of(others[d]),
            device_id_type=MESH,
        )

    copies = [copy_of(x_ref.at[other], land.at[d], 0, d) for d, other in enumerate(others)]
    for copy in copies:
        copy.start()
    total = x_ref[me]
    for d, copy in enumerate(copies):
        copy.wait_recv()
        total = total + land[d]
    out_ref[me] = total
    spreads = [copy_of(out_ref.at[me], out_ref.at[me], 1, d) for d in range(count - 1)]
    for copy in spreads:
        copy.start()
    for copy in copies:
        copy.wait_send()
    for d in range(count - 1):
        source = lax.rem(me + count - 1 - d, count)
        copy_of(out_ref.at[me], out_ref.at[source], 1, d).wait_recv()
    for copy in spreads:
        copy.wait_send()


def summed(block):
    count = lax.axis_size(LINE)
    rows = block.shape[0]
    each = -(-rows // (count * SUB)) * SUB
    padded = jnp.pad(block, ((0, each * count - rows), (0, 0))).reshape(count, each, LANES)
    vmem = pl.BlockSpec(memory_space=pltpu.VMEM)
    result = pl.pallas_call(
        sum_kernel,
        in_specs=[vmem],
        out_specs=vmem,
        out_shape=jax.ShapeDtypeStruct(padded.shape, jnp.float32),
        scratch_shapes=[
            pltpu.VMEM((count - 1, each, LANES), jnp.float32),
            pltpu.SemaphoreType.DMA((2, count - 1)),
            pltpu.SemaphoreType.DMA((2, count - 1)),
        ],
        compiler_params=pltpu.CompilerParams(
            collective_id=1, has_side_effects=True, vmem_limit_bytes=16 * 1024 * 1024
        ),
        name="sums",
    )(padded)
    return result.reshape(count * each, LANES)[:rows]


def tiles(block):
    lead, sub, chans = block.shape
    return block.reshape(lead, sub, chans // LANES, LANES).transpose(0, 2, 1, 3).reshape(-1, LANES)


def untiled(flat, lead, sub, chans):
    return flat.reshape(lead, chans // LANES, sub, LANES).transpose(0, 2, 1, 3).reshape(lead, sub, chans)


def spread_matrix(local_groups, width, members):
    first = pl.program_id(0) * width
    row = lax.broadcasted_iota(jnp.int32, (local_groups, width), 0)
    col = lax.broadcasted_iota(jnp.int32, (local_groups, width), 1) + first
    low = row * members
    return jnp.where((col >= low) & (col < low + members), 1.0, 0.0).astype(jnp.float32)


def first_kernel(members, q_ref, k_ref, v_ref, g_ref, prev_ref, next_ref, taps_ref, rate_ref, res_ref,
                 mix_ref, ef_ref, ea_ref, final_ref, first_ref, rates_ref, ress_ref, wide, src, adj, each):
    rows, width = q_ref.shape
    modes, local_groups = rate_ref.shape
    tap_count = taps_ref.shape[1]
    steps = rows // SUB
    onto = spread_matrix(local_groups, width, members)
    rates_ref[...] = jnp.dot(rate_ref[...], onto, precision=EXACT, preferred_element_type=jnp.float32)
    ress_ref[...] = jnp.dot(res_ref[...], onto, precision=EXACT, preferred_element_type=jnp.float32)
    for i, x_ref in enumerate((q_ref, k_ref, v_ref)):
        wide[i, 0:SUB] = prev_ref[i]
        wide[i, SUB:SUB + rows] = x_ref[...].astype(jnp.float32)
        wide[i, SUB + rows:] = next_ref[i]
    chunk = lax.broadcasted_iota(jnp.int32, (SUB, LANES), 0).astype(jnp.float32)

    @pl.loop(0, width // LANES)
    def _(column):
        cols = pl.ds(pl.multiple_of(column * LANES, LANES), LANES)
        mixes = []
        for i in range(3):
            total = taps_ref[i, 0:1, cols] * wide[i, SUB:, cols]
            for j in range(1, tap_count):
                total = total + taps_ref[i, j:j + 1, cols] * wide[i, SUB - j:2 * SUB + rows - j, cols]
            mix_ref[i, :, cols] = total
            mixes.append(total[:rows])
        src[:, :] = mixes[1] * mixes[2]
        adj[:, :] = mixes[0] * g_ref[:, cols].astype(jnp.float32)
        s = [src[pl.ds(j, SUB, stride=steps), :] for j in range(steps)]
        a = [adj[pl.ds(j, SUB, stride=steps), :] for j in range(steps)]

        for n in range(modes):
            each[0, n] = jnp.broadcast_to(rates_ref[n:n + 1, cols], (SUB, LANES))

        def one(n, nothing):
            rate = each[0, n]
            lam = jnp.exp(-rate)
            ahead = s[0]
            back = a[steps - 1]
            for j in range(1, steps):
                ahead = lam * ahead + s[j]
                back = lam * back + a[steps - 1 - j]
            ef_ref[n, :, cols] = ahead
            ea_ref[n, :, cols] = back
            later = jnp.exp(rate * ((chunk - (SUB - 1)) * float(steps)))
            sooner = jnp.exp(rate * (chunk * -float(steps)))
            each[1, n] = ahead * later
            each[2, n] = back * sooner
            return nothing

        lax.fori_loop(0, modes, one, 0, unroll=4)
        final_ref[:, cols] = jnp.sum(each[1], axis=1)
        first_ref[:, cols] = jnp.sum(each[2], axis=1)


def second_kernel(members, q_ref, k_ref, v_ref, g_ref, prev_ref, gnext_ref, taps_ref, mix_ref, ef_ref, ea_ref,
                  final_ref, rates_ref, ress_ref, sin_ref, pin_ref,
                  qg_ref, kg_ref, vg_ref, tap_ref, mode_ref, pole_ref,
                  wide, src, adj, long_out, long_adj, back, mode_rows, pole_rows, each, sums, terms, held):
    rows, width = q_ref.shape
    modes = rates_ref.shape[0]
    local_groups = mode_ref.shape[1]
    tap_count = taps_ref.shape[1]
    steps = rows // SUB
    for i, x_ref in enumerate((q_ref, k_ref, v_ref)):
        wide[i, 0:SUB] = prev_ref[i]
        wide[i, SUB:] = x_ref[...].astype(jnp.float32)
    chunk = lax.broadcasted_iota(jnp.int32, (SUB, LANES), 0)

    @pl.loop(0, width // LANES)
    def _(column):
        cols = pl.ds(pl.multiple_of(column * LANES, LANES), LANES)
        src[:, :] = mix_ref[1, :, cols] * mix_ref[2, :, cols]
        adj[:rows, :] = mix_ref[0, :rows, cols] * g_ref[:, cols].astype(jnp.float32)
        adj[rows:, :] = mix_ref[0, rows:, cols] * gnext_ref[:, cols]
        s = [src[pl.ds(j, SUB, stride=steps), :] for j in range(steps)]
        a = [adj[pl.ds(j, SUB, stride=steps), :] for j in range(steps)]
        zero = jnp.zeros((SUB, LANES), jnp.float32)

        lam_table = jnp.exp(-rates_ref[:, cols])
        decay_table = jnp.exp(rates_ref[:, cols] * -float(steps))
        for i, table in enumerate((lam_table, ress_ref[:, cols])):
            for n in range(modes):
                each[i, n] = jnp.broadcast_to(table[n:n + 1], (SUB, LANES))
        for n in range(modes):
            decay = jnp.broadcast_to(decay_table[n:n + 1], (SUB, LANES))
            state = jnp.where(chunk == 0, sin_ref[n:n + 1, cols], pltpu.roll(ef_ref[n, :, cols], 1, 0))
            late = jnp.where(
                chunk == SUB - 1, pin_ref[n:n + 1, cols], pltpu.roll(ea_ref[n, :, cols], SUB - 1, 0)
            )
            distance = 1
            while distance < SUB:
                state = state + jnp.where(chunk >= distance, decay * pltpu.roll(state, distance, 0), 0.0)
                late = late + jnp.where(chunk < SUB - distance, decay * pltpu.roll(late, SUB - distance, 0), 0.0)
                decay = decay * decay
                distance *= 2
            each[2, n] = state
            each[3, n] = late
        for j in range(steps):
            sums[0, j] = zero
            sums[1, j] = zero
            terms[0, j] = s[j]
            terms[1, j] = a[j]

        @pl.loop(0, modes // TOGETHER)
        def _(group):
            here = [group * TOGETHER + m for m in range(TOGETHER)]
            lam = [each[0, n] for n in here]
            res = [each[1, n] for n in here]
            state = [each[2, n] for n in here]
            late = [each[3, n] for n in here]
            mode_sum = [zero] * TOGETHER
            pole_sum = [zero] * TOGETHER
            for j in range(steps):
                source, toward, out = terms[0, j], terms[1, j], sums[0, j]
                for m in range(TOGETHER):
                    held[m, j] = state[m]
                    state[m] = lam[m] * state[m] + source
                    out = out + res[m] * state[m]
                    mode_sum[m] = mode_sum[m] + toward * state[m]
                sums[0, j] = out
            for j in range(steps - 1, -1, -1):
                toward, out = terms[1, j], sums[1, j]
                for m in range(TOGETHER):
                    late[m] = lam[m] * late[m] + toward
                    out = out + res[m] * late[m]
                    pole_sum[m] = pole_sum[m] + late[m] * held[m, j]
                sums[1, j] = out
            for m, n in enumerate(here):
                each[4, n] = mode_sum[m]
                each[5, n] = lam[m] * res[m] * pole_sum[m]

        mode_rows[:, cols] = jnp.sum(each[4], axis=1)
        pole_rows[:, cols] = jnp.sum(each[5], axis=1)
        for j in range(steps):
            long_out[pl.ds(j, SUB, stride=steps), :] = sums[0, j]
            long_adj[pl.ds(j, SUB, stride=steps), :] = sums[1, j]
        rate = rates_ref[:, cols]
        res = ress_ref[:, cols]
        lam = jnp.exp(-rate)
        grow = jnp.exp(rate)
        state = jnp.exp(rate * -float(rows)) * sin_ref[:, cols] + final_ref[:, cols]
        late = pin_ref[:, cols]
        long_out[rows:, :] = zero
        long_adj[rows:, :] = zero
        for j in range(tap_count - 1):
            state = lam * state + src[rows + j:rows + j + 1, :]
            long_out[rows + j:rows + j + 1, :] = jnp.sum(res * state, axis=0, keepdims=True)
            long_adj[rows + j:rows + j + 1, :] = jnp.sum(res * late, axis=0, keepdims=True)
            late = (late - adj[rows + j:rows + j + 1, :]) * grow
        back[0, :rows, cols] = g_ref[:, cols].astype(jnp.float32) * long_out[:rows, :]
        back[0, rows:, cols] = gnext_ref[:, cols] * long_out[rows:, :]
        back[1, :, cols] = long_adj[:, :] * mix_ref[2, :, cols]
        back[2, :, cols] = long_adj[:, :] * mix_ref[1, :, cols]
        for i, grad_ref in enumerate((qg_ref, kg_ref, vg_ref)):
            mine = back[i, 0:rows, cols]
            total = taps_ref[i, 0:1, cols] * mine
            for j in range(1, tap_count):
                total = total + taps_ref[i, j:j + 1, cols] * back[i, j:j + rows, cols]
            grad_ref[:, cols] = total.astype(grad_ref.dtype)
            for j in range(tap_count):
                tap_ref[i, j:j + 1, cols] = jnp.sum(
                    mine * wide[i, SUB - j:SUB - j + rows, cols], axis=0, keepdims=True
                )
            for j in range(tap_count, SUB):
                tap_ref[i, j:j + 1, cols] = jnp.zeros((1, LANES), jnp.float32)

    onto = spread_matrix(local_groups, width, members)
    along = (((1,), (1,)), ((), ()))

    @pl.when(pl.program_id(0) == 0)
    def _():
        mode_ref[...] = jnp.zeros_like(mode_ref)
        pole_ref[...] = jnp.zeros_like(pole_ref)

    mode_ref[...] += lax.dot_general(
        mode_rows[...], onto, along, precision=EXACT, preferred_element_type=jnp.float32
    )
    pole_ref[...] += lax.dot_general(
        pole_rows[...], onto, along, precision=EXACT, preferred_element_type=jnp.float32
    )


def on_device(queries, keys_in, values_in, out_grad, short_taps, pole_rate, residue):
    rows, chans = queries.shape
    modes, local_groups = pole_rate.shape
    members = chans // local_groups
    tap_count = short_taps.shape[1]
    token_total = rows * lax.axis_size(LINE)
    width = min(512, chans)
    f32 = jnp.float32
    tails = jnp.stack([x[rows - SUB:] for x in (queries, keys_in, values_in)])
    heads = jnp.stack([x[:SUB] for x in (queries, keys_in, values_in, out_grad)])
    before = moved(tails, 1).astype(f32)
    after = moved(heads, -1).astype(f32)

    def cut(*lead):
        zeros = (0,) * len(lead)
        return pl.BlockSpec((*lead, width), lambda i: (*zeros, i))

    def full(*shape):
        zeros = (0,) * len(shape)
        return pl.BlockSpec(shape, lambda i: zeros)

    def arr(*shape, dtype=f32):
        return jax.ShapeDtypeStruct(shape, dtype)

    params = pltpu.CompilerParams(vmem_limit_bytes=48 * 1024 * 1024)
    wide_rows = rows + SUB
    streams = [cut(rows)] * 4
    mix, ef, ea, final, first, rates, ress = pl.pallas_call(
        functools.partial(first_kernel, members),
        grid=(chans // width,),
        in_specs=streams + [
            cut(3, SUB), cut(3, SUB), cut(3, tap_count), full(modes, local_groups), full(modes, local_groups)
        ],
        out_specs=[cut(3, wide_rows), cut(modes, SUB), cut(modes, SUB)] + [cut(modes)] * 4,
        out_shape=[arr(3, wide_rows, chans), arr(modes, SUB, chans), arr(modes, SUB, chans)]
        + [arr(modes, chans)] * 4,
        scratch_shapes=[
            pltpu.VMEM((3, wide_rows + SUB, width), f32),
            pltpu.VMEM((rows, LANES), f32),
            pltpu.VMEM((rows, LANES), f32),
            pltpu.VMEM((3, modes, SUB, LANES), f32),
        ],
        compiler_params=params,
        name="local_states",
    )(queries, keys_in, values_in, out_grad, before, after[:3], short_taps, pole_rate, residue)
    state_in, late_in = carried(final, first, rates, rows)
    query_grad, key_grad, value_grad, taps_sum, mode_sum, pole_sum = pl.pallas_call(
        functools.partial(second_kernel, members),
        grid=(chans // width,),
        in_specs=streams + [
            cut(3, SUB), cut(SUB), cut(3, tap_count), cut(3, wide_rows), cut(modes, SUB), cut(modes, SUB)
        ] + [cut(modes)] * 5,
        out_specs=[cut(rows)] * 3 + [cut(3, SUB), full(modes, local_groups), full(modes, local_groups)],
        out_shape=[arr(rows, chans, dtype=jnp.bfloat16)] * 3
        + [arr(3, SUB, chans), arr(modes, local_groups), arr(modes, local_groups)],
        scratch_shapes=[pltpu.VMEM((3, wide_rows, width), f32)]
        + [pltpu.VMEM((wide_rows, LANES), f32)] * 4
        + [pltpu.VMEM((3, wide_rows, width), f32)]
        + [pltpu.VMEM((modes, width), f32)] * 2
        + [pltpu.VMEM((6, modes, SUB, LANES), f32)]
        + [pltpu.VMEM((2, rows // SUB, SUB, LANES), f32)] * 2
        + [pltpu.VMEM((TOGETHER, rows // SUB, SUB, LANES), f32)],
        compiler_params=params,
        name="gradients",
    )(queries, keys_in, values_in, out_grad, before, after[3], short_taps, mix, ef, ea,
      final, rates, ress, state_in, late_in)
    taps_sum, mode_sum, pole_sum = summed_all(taps_sum, mode_sum, pole_sum)
    tap_grad = taps_sum[:, :tap_count] / jnp.sqrt(f32(token_total))
    return (query_grad, key_grad, value_grad, tap_grad, -pole_sum / f32(token_total), mode_sum / f32(token_total))


def summed_all(taps_sum, mode_sum, pole_sum):
    modes, groups = mode_sum.shape
    blocks = [taps_sum] + [x.reshape(modes // SUB, SUB, groups) for x in (mode_sum, pole_sum)]
    parts = [tiles(x) for x in blocks]
    total = summed(jnp.concatenate(parts, axis=0))
    results, start = [], 0
    for part, block in zip(parts, blocks):
        results.append(untiled(total[start:start + part.shape[0]], *block.shape))
        start += part.shape[0]
    return results[0], results[1].reshape(modes, groups), results[2].reshape(modes, groups)


def solution(mesh):
    tokens = P(("groups", "ctx", "inner"), "chan")
    return jax.shard_map(
        on_device,
        mesh=mesh,
        in_specs=(tokens, tokens, tokens, tokens, P(None, None, "chan"), P(None, "chan"), P(None, "chan")),
        out_specs=(
            tokens,
            tokens,
            tokens,
            P("groups", None, "chan"),
            P("groups", "chan"),
            P("groups", "chan"),
        ),
        check_vma=False,
    )
```

```python
import functools

import jax
import jax.numpy as jnp
from jax import lax
from jax.experimental import pallas as pl
from jax.experimental.pallas import tpu as pltpu
from jax.sharding import PartitionSpec as P

LINE = ("ctx", "inner")
LANES = 128
SUB = 8
TOGETHER = 8
PIECE = 1024
MESH = pl.DeviceIdType.MESH


def moved(block, distance):
    devices = range(lax.axis_size(LINE))
    return lax.ppermute(block, LINE, [(i, i + distance) for i in devices if i + distance in devices])


def place_of(position):
    inner = lax.axis_size("inner")
    return {"ctx": position // inner, "inner": position % inner}


def carry_kernel(pieces, rows, final_ref, first_ref, rates_ref, sin_ref, pin_ref, near, outward, entering,
                 near_send, near_recv, far_send, far_recv, give_send, give_recv):
    inner, outer = lax.axis_size("inner"), lax.axis_size("ctx")
    x, z = lax.axis_index("inner"), lax.axis_index("ctx")
    width = final_ref.shape[1] // pieces
    barrier = pltpu.get_barrier_semaphore()
    others = [lax.rem(x + d, inner) for d in range(1, inner)]
    for other in others:
        pl.semaphore_signal(barrier, inc=1, device_id={"inner": other}, device_id_type=MESH)

    @pl.when(z > 0)
    def _():
        pl.semaphore_signal(barrier, inc=1, device_id={"ctx": z - 1}, device_id_type=MESH)

    @pl.when(z < outer - 1)
    def _():
        pl.semaphore_signal(barrier, inc=1, device_id={"ctx": z + 1}, device_id_type=MESH)

    pl.semaphore_wait(barrier, inner - 1 + jnp.where(z > 0, 1, 0) + jnp.where(z < outer - 1, 1, 0))

    def copy(source, target, send, recv, where):
        return pltpu.make_async_remote_copy(
            src_ref=source, dst_ref=target, send_sem=send, recv_sem=recv, device_id=where, device_id_type=MESH
        )

    lines = []
    for line, total_ref, into_ref in ((0, final_ref, sin_ref), (1, first_ref, pin_ref)):
        xs, zs = (x, z) if line == 0 else (inner - 1 - x, outer - 1 - z)
        lines.append((line, total_ref, into_ref, xs, zs, 1 if line == 0 else -1))

    def near_copy(line, total_ref, piece, steps, sign):
        cols = pl.ds(piece * width, width)
        return copy(
            total_ref.at[:, cols], near.at[line, steps - 1, :, cols],
            near_send.at[line, steps - 1, piece], near_recv.at[line, steps - 1, piece],
            {"inner": lax.rem(x + sign * steps + inner, inner)},
        )

    def far_copy(line, piece, sign):
        cols = pl.ds(piece * width, width)
        return copy(
            outward.at[line, :, cols], entering.at[line, :, cols],
            far_send.at[line, piece], far_recv.at[line, piece],
            {"ctx": lax.rem(z + sign + outer, outer)},
        )

    def give_copy(line, piece, steps, sign):
        cols = pl.ds(piece * width, width)
        return copy(
            entering.at[line, :, cols], entering.at[line, :, cols],
            give_send.at[line, steps - 1, piece], give_recv.at[line, piece],
            {"inner": lax.rem(x - sign * steps + inner, inner)},
        )

    for piece in range(pieces):
        for line, total_ref, _, xs, _, sign in lines:
            for steps in range(1, inner):
                @pl.when(xs + steps < inner)
                def _():
                    near_copy(line, total_ref, piece, steps, sign).start()

    for piece in range(pieces):
        cols = pl.ds(piece * width, width)
        decay = jnp.exp(rates_ref[:, cols] * -float(rows))
        for line, total_ref, into_ref, xs, zs, sign in lines:
            @pl.when(xs == inner - 1)
            def _():
                total = jnp.zeros_like(into_ref[:, cols])
                for steps in range(inner - 1, 0, -1):
                    near_copy(line, total_ref, piece, steps, sign).wait_recv()
                    total = decay * total + near[line, steps - 1, :, cols]
                into_ref[:, cols] = total

                @pl.when(zs == 0)
                def _():
                    entering[line, :, cols] = jnp.zeros_like(total)

                @pl.when(zs > 0)
                def _():
                    far_copy(line, piece, sign).wait_recv()

                power = jnp.exp(rates_ref[:, cols] * -float(rows * (inner - 1)))
                mine = power * entering[line, :, cols] + into_ref[:, cols]
                into_ref[:, cols] = mine

                @pl.when(zs < outer - 1)
                def _():
                    outward[line, :, cols] = decay * mine + total_ref[:, cols]
                    far_copy(line, piece, sign).start()

                for steps in range(1, inner):
                    give_copy(line, piece, steps, sign).start()

    for piece in range(pieces):
        cols = pl.ds(piece * width, width)
        decay = jnp.exp(rates_ref[:, cols] * -float(rows))
        for line, total_ref, into_ref, xs, zs, sign in lines:
            @pl.when(xs < inner - 1)
            def _():
                into_ref[:, cols] = jnp.zeros_like(into_ref[:, cols])
                for steps in range(inner - 2, 0, -1):
                    @pl.when(xs >= steps)
                    def _():
                        near_copy(line, total_ref, piece, steps, sign).wait_recv()
                        into_ref[:, cols] = decay * into_ref[:, cols] + near[line, steps - 1, :, cols]

                give_copy(line, piece, 1, sign).wait_recv()
                power = jnp.exp(rates_ref[:, cols] * (-float(rows) * xs.astype(jnp.float32)))
                into_ref[:, cols] = power * entering[line, :, cols] + into_ref[:, cols]

    for piece in range(pieces):
        for line, total_ref, _, xs, zs, sign in lines:
            for steps in range(1, inner):
                @pl.when(xs + steps < inner)
                def _():
                    near_copy(line, total_ref, piece, steps, sign).wait_send()

                @pl.when(xs == inner - 1)
                def _():
                    give_copy(line, piece, steps, sign).wait_send()

            @pl.when((xs == inner - 1) & (zs < outer - 1))
            def _():
                far_copy(line, piece, sign).wait_send()


def carried(final, first, rates, rows):
    modes, chans = final.shape
    pieces = max(1, chans // PIECE)
    hops = max(1, lax.axis_size("inner") - 1)
    shape = jax.ShapeDtypeStruct((modes, chans), jnp.float32)
    vmem = pl.BlockSpec(memory_space=pltpu.VMEM)
    return pl.pallas_call(
        functools.partial(carry_kernel, pieces, rows),
        in_specs=[vmem] * 3,
        out_specs=[vmem] * 2,
        out_shape=[shape] * 2,
        scratch_shapes=[
            pltpu.VMEM((2, hops, modes, chans), jnp.float32),
            pltpu.VMEM((2, modes, chans), jnp.float32),
            pltpu.VMEM((2, modes, chans), jnp.float32),
            pltpu.SemaphoreType.DMA((2, hops, pieces)),
            pltpu.SemaphoreType.DMA((2, hops, pieces)),
            pltpu.SemaphoreType.DMA((2, pieces)),
            pltpu.SemaphoreType.DMA((2, pieces)),
            pltpu.SemaphoreType.DMA((2, hops, pieces)),
            pltpu.SemaphoreType.DMA((2, pieces)),
        ],
        compiler_params=pltpu.CompilerParams(
            collective_id=0, has_side_effects=True, vmem_limit_bytes=16 * 1024 * 1024
        ),
        name="carry",
    )(final, first, rates)


def sum_kernel(x_ref, out_ref, land, send_sem, recv_sem):
    count = lax.axis_size(LINE)
    me = lax.axis_index("ctx") * lax.axis_size("inner") + lax.axis_index("inner")
    barrier = pltpu.get_barrier_semaphore()
    others = [lax.rem(me + d, count) for d in range(1, count)]
    for other in others:
        pl.semaphore_signal(barrier, inc=1, device_id=place_of(other), device_id_type=MESH)
    pl.semaphore_wait(barrier, count - 1)

    def copy_of(source, target, phase, d):
        return pltpu.make_async_remote_copy(
            src_ref=source,
            dst_ref=target,
            send_sem=send_sem.at[phase, d],
            recv_sem=recv_sem.at[phase, d],
            device_id=place_of(others[d]),
            device_id_type=MESH,
        )

    copies = [copy_of(x_ref.at[other], land.at[d], 0, d) for d, other in enumerate(others)]
    for copy in copies:
        copy.start()
    total = x_ref[me]
    for d, copy in enumerate(copies):
        copy.wait_recv()
        total = total + land[d]
    out_ref[me] = total
    spreads = [copy_of(out_ref.at[me], out_ref.at[me], 1, d) for d in range(count - 1)]
    for copy in spreads:
        copy.start()
    for copy in copies:
        copy.wait_send()
    for d in range(count - 1):
        source = lax.rem(me + count - 1 - d, count)
        copy_of(out_ref.at[me], out_ref.at[source], 1, d).wait_recv()
    for copy in spreads:
        copy.wait_send()


def summed(block):
    count = lax.axis_size(LINE)
    rows = block.shape[0]
    each = -(-rows // (count * SUB)) * SUB
    padded = jnp.pad(block, ((0, each * count - rows), (0, 0))).reshape(count, each, LANES)
    vmem = pl.BlockSpec(memory_space=pltpu.VMEM)
    result = pl.pallas_call(
        sum_kernel,
        in_specs=[vmem],
        out_specs=vmem,
        out_shape=jax.ShapeDtypeStruct(padded.shape, jnp.float32),
        scratch_shapes=[
            pltpu.VMEM((count - 1, each, LANES), jnp.float32),
            pltpu.SemaphoreType.DMA((2, count - 1)),
            pltpu.SemaphoreType.DMA((2, count - 1)),
        ],
        compiler_params=pltpu.CompilerParams(
            collective_id=1, has_side_effects=True, vmem_limit_bytes=16 * 1024 * 1024
        ),
        name="sums",
    )(padded)
    return result.reshape(count * each, LANES)[:rows]


def tiles(block):
    lead, sub, chans = block.shape
    return block.reshape(lead, sub, chans // LANES, LANES).transpose(0, 2, 1, 3).reshape(-1, LANES)


def untiled(flat, lead, sub, chans):
    return flat.reshape(lead, chans // LANES, sub, LANES).transpose(0, 2, 1, 3).reshape(lead, sub, chans)


def spread_matrix(local_groups, width, members, over_rows):
    shape = (width, local_groups) if over_rows else (local_groups, width)
    chan = lax.broadcasted_iota(jnp.int32, shape, 0 if over_rows else 1) + pl.program_id(0) * width
    low = lax.broadcasted_iota(jnp.int32, shape, 1 if over_rows else 0) * members
    return jnp.where((chan >= low) & (chan < low + members), 1.0, 0.0).astype(jnp.bfloat16)


def table_dots(tables, onto):
    terms = []
    for rest in tables:
        for _ in range(3):
            term = rest.astype(jnp.bfloat16)
            terms.append(term)
            rest = rest - term.astype(jnp.float32)
    rows = tables[0].shape[0]
    out = jnp.dot(jnp.concatenate(terms, axis=0), onto, preferred_element_type=jnp.float32)
    cut = [out[i * rows:(i + 1) * rows] for i in range(len(terms))]
    return [cut[3 * i] + cut[3 * i + 1] + cut[3 * i + 2] for i in range(len(tables))]


def first_kernel(members, q_ref, k_ref, v_ref, g_ref, prev_ref, next_ref, taps_ref, rate_ref, res_ref,
                 mix_ref, ef_ref, ea_ref, final_ref, first_ref, rates_ref, ress_ref, wide, src, adj, each):
    rows, width = q_ref.shape
    modes, local_groups = rate_ref.shape
    tap_count = taps_ref.shape[1]
    steps = rows // SUB
    onto = spread_matrix(local_groups, width, members, False)
    rates_ref[...], ress_ref[...] = table_dots([rate_ref[...], res_ref[...]], onto)
    for i, x_ref in enumerate((q_ref, k_ref, v_ref)):
        wide[i, 0:SUB] = prev_ref[i]
        wide[i, SUB:SUB + rows] = x_ref[...].astype(jnp.float32)
        wide[i, SUB + rows:] = next_ref[i]
    chunk = lax.broadcasted_iota(jnp.int32, (SUB, LANES), 0).astype(jnp.float32)

    @pl.loop(0, width // LANES)
    def _(column):
        cols = pl.ds(pl.multiple_of(column * LANES, LANES), LANES)
        mixes = []
        for i in range(3):
            total = taps_ref[i, 0:1, cols] * wide[i, SUB:, cols]
            for j in range(1, tap_count):
                total = total + taps_ref[i, j:j + 1, cols] * wide[i, SUB - j:2 * SUB + rows - j, cols]
            mix_ref[i, :, cols] = total
            mixes.append(total[:rows])
        src[:, :] = mixes[1] * mixes[2]
        adj[:, :] = mixes[0] * g_ref[:, cols].astype(jnp.float32)
        s = [src[pl.ds(j, SUB, stride=steps), :] for j in range(steps)]
        a = [adj[pl.ds(j, SUB, stride=steps), :] for j in range(steps)]

        for n in range(modes):
            each[0, n] = jnp.broadcast_to(rates_ref[n:n + 1, cols], (SUB, LANES))

        def one(n, nothing):
            rate = each[0, n]
            lam = jnp.exp(-rate)
            ahead = s[0]
            back = a[steps - 1]
            for j in range(1, steps):
                ahead = lam * ahead + s[j]
                back = lam * back + a[steps - 1 - j]
            ef_ref[n, :, cols] = ahead
            ea_ref[n, :, cols] = back
            later = jnp.exp(rate * ((chunk - (SUB - 1)) * float(steps)))
            sooner = jnp.exp(rate * (chunk * -float(steps)))
            each[1, n] = ahead * later
            each[2, n] = back * sooner
            return nothing

        lax.fori_loop(0, modes, one, 0, unroll=4)
        final_ref[:, cols] = jnp.sum(each[1], axis=1)
        first_ref[:, cols] = jnp.sum(each[2], axis=1)


def second_kernel(members, q_ref, k_ref, v_ref, g_ref, prev_ref, gnext_ref, taps_ref, mix_ref, ef_ref, ea_ref,
                  final_ref, rates_ref, ress_ref, sin_ref, pin_ref,
                  qg_ref, kg_ref, vg_ref, tap_ref, mode_ref, pole_ref,
                  wide, src, adj, long_out, long_adj, back, mode_rows, pole_rows, each, sums, terms, held):
    rows, width = q_ref.shape
    modes = rates_ref.shape[0]
    local_groups = mode_ref.shape[1]
    tap_count = taps_ref.shape[1]
    steps = rows // SUB
    for i, x_ref in enumerate((q_ref, k_ref, v_ref)):
        wide[i, 0:SUB] = prev_ref[i]
        wide[i, SUB:] = x_ref[...].astype(jnp.float32)
    chunk = lax.broadcasted_iota(jnp.int32, (SUB, LANES), 0)

    @pl.loop(0, width // LANES)
    def _(column):
        cols = pl.ds(pl.multiple_of(column * LANES, LANES), LANES)
        src[:, :] = mix_ref[1, :, cols] * mix_ref[2, :, cols]
        adj[:rows, :] = mix_ref[0, :rows, cols] * g_ref[:, cols].astype(jnp.float32)
        adj[rows:, :] = mix_ref[0, rows:, cols] * gnext_ref[:, cols]
        s = [src[pl.ds(j, SUB, stride=steps), :] for j in range(steps)]
        a = [adj[pl.ds(j, SUB, stride=steps), :] for j in range(steps)]
        zero = jnp.zeros((SUB, LANES), jnp.float32)

        lam_table = jnp.exp(-rates_ref[:, cols])
        decay_table = jnp.exp(rates_ref[:, cols] * -float(steps))
        for i, table in enumerate((lam_table, ress_ref[:, cols])):
            for n in range(modes):
                each[i, n] = jnp.broadcast_to(table[n:n + 1], (SUB, LANES))
        for n in range(modes):
            decay = jnp.broadcast_to(decay_table[n:n + 1], (SUB, LANES))
            state = jnp.where(chunk == 0, sin_ref[n:n + 1, cols], pltpu.roll(ef_ref[n, :, cols], 1, 0))
            late = jnp.where(
                chunk == SUB - 1, pin_ref[n:n + 1, cols], pltpu.roll(ea_ref[n, :, cols], SUB - 1, 0)
            )
            distance = 1
            while distance < SUB:
                state = state + jnp.where(chunk >= distance, decay * pltpu.roll(state, distance, 0), 0.0)
                late = late + jnp.where(chunk < SUB - distance, decay * pltpu.roll(late, SUB - distance, 0), 0.0)
                decay = decay * decay
                distance *= 2
            each[2, n] = state
            each[3, n] = late
        for j in range(steps):
            sums[0, j] = zero
            sums[1, j] = zero
            terms[0, j] = s[j]
            terms[1, j] = a[j]

        @pl.loop(0, modes // TOGETHER)
        def _(group):
            here = [group * TOGETHER + m for m in range(TOGETHER)]
            lam = [each[0, n] for n in here]
            res = [each[1, n] for n in here]
            state = [each[2, n] for n in here]
            late = [each[3, n] for n in here]
            mode_sum = [zero] * TOGETHER
            pole_sum = [zero] * TOGETHER
            for j in range(steps):
                source, toward, out = terms[0, j], terms[1, j], sums[0, j]
                for m in range(TOGETHER):
                    held[m, j] = state[m]
                    state[m] = lam[m] * state[m] + source
                    out = out + res[m] * state[m]
                    mode_sum[m] = mode_sum[m] + toward * state[m]
                sums[0, j] = out
            for j in range(steps - 1, -1, -1):
                toward, out = terms[1, j], sums[1, j]
                for m in range(TOGETHER):
                    late[m] = lam[m] * late[m] + toward
                    out = out + res[m] * late[m]
                    pole_sum[m] = pole_sum[m] + late[m] * held[m, j]
                sums[1, j] = out
            for m, n in enumerate(here):
                each[4, n] = mode_sum[m]
                each[5, n] = lam[m] * res[m] * pole_sum[m]

        mode_rows[:, cols] = jnp.sum(each[4], axis=1)
        pole_rows[:, cols] = jnp.sum(each[5], axis=1)
        for j in range(steps):
            long_out[pl.ds(j, SUB, stride=steps), :] = sums[0, j]
            long_adj[pl.ds(j, SUB, stride=steps), :] = sums[1, j]
        rate = rates_ref[:, cols]
        res = ress_ref[:, cols]
        lam = jnp.exp(-rate)
        grow = jnp.exp(rate)
        state = jnp.exp(rate * -float(rows)) * sin_ref[:, cols] + final_ref[:, cols]
        late = pin_ref[:, cols]
        long_out[rows:, :] = zero
        long_adj[rows:, :] = zero
        for j in range(tap_count - 1):
            state = lam * state + src[rows + j:rows + j + 1, :]
            long_out[rows + j:rows + j + 1, :] = jnp.sum(res * state, axis=0, keepdims=True)
            long_adj[rows + j:rows + j + 1, :] = jnp.sum(res * late, axis=0, keepdims=True)
            late = (late - adj[rows + j:rows + j + 1, :]) * grow
        back[0, :rows, cols] = g_ref[:, cols].astype(jnp.float32) * long_out[:rows, :]
        back[0, rows:, cols] = gnext_ref[:, cols] * long_out[rows:, :]
        back[1, :, cols] = long_adj[:, :] * mix_ref[2, :, cols]
        back[2, :, cols] = long_adj[:, :] * mix_ref[1, :, cols]
        for i, grad_ref in enumerate((qg_ref, kg_ref, vg_ref)):
            mine = back[i, 0:rows, cols]
            total = taps_ref[i, 0:1, cols] * mine
            for j in range(1, tap_count):
                total = total + taps_ref[i, j:j + 1, cols] * back[i, j:j + rows, cols]
            grad_ref[:, cols] = total.astype(grad_ref.dtype)
            for j in range(tap_count):
                tap_ref[i, j:j + 1, cols] = jnp.sum(
                    mine * wide[i, SUB - j:SUB - j + rows, cols], axis=0, keepdims=True
                )
            for j in range(tap_count, SUB):
                tap_ref[i, j:j + 1, cols] = jnp.zeros((1, LANES), jnp.float32)

    onto = spread_matrix(local_groups, width, members, True)
    mode_part, pole_part = table_dots([mode_rows[...], pole_rows[...]], onto)

    @pl.when(pl.program_id(0) == 0)
    def _():
        mode_ref[...] = jnp.zeros_like(mode_ref)
        pole_ref[...] = jnp.zeros_like(pole_ref)

    mode_ref[...] += mode_part
    pole_ref[...] += pole_part


def on_device(queries, keys_in, values_in, out_grad, short_taps, pole_rate, residue):
    rows, chans = queries.shape
    modes, local_groups = pole_rate.shape
    members = chans // local_groups
    tap_count = short_taps.shape[1]
    token_total = rows * lax.axis_size(LINE)
    width = min(512, chans)
    f32 = jnp.float32
    tails = jnp.stack([x[rows - SUB:] for x in (queries, keys_in, values_in)])
    heads = jnp.stack([x[:SUB] for x in (queries, keys_in, values_in, out_grad)])
    before = moved(tails, 1).astype(f32)
    after = moved(heads, -1).astype(f32)

    def cut(*lead):
        zeros = (0,) * len(lead)
        return pl.BlockSpec((*lead, width), lambda i: (*zeros, i))

    def full(*shape):
        zeros = (0,) * len(shape)
        return pl.BlockSpec(shape, lambda i: zeros)

    def arr(*shape, dtype=f32):
        return jax.ShapeDtypeStruct(shape, dtype)

    params = pltpu.CompilerParams(vmem_limit_bytes=48 * 1024 * 1024)
    wide_rows = rows + SUB
    streams = [cut(rows)] * 4
    mix, ef, ea, final, first, rates, ress = pl.pallas_call(
        functools.partial(first_kernel, members),
        grid=(chans // width,),
        in_specs=streams + [
            cut(3, SUB), cut(3, SUB), cut(3, tap_count), full(modes, local_groups), full(modes, local_groups)
        ],
        out_specs=[cut(3, wide_rows), cut(modes, SUB), cut(modes, SUB)] + [cut(modes)] * 4,
        out_shape=[arr(3, wide_rows, chans), arr(modes, SUB, chans), arr(modes, SUB, chans)]
        + [arr(modes, chans)] * 4,
        scratch_shapes=[
            pltpu.VMEM((3, wide_rows + SUB, width), f32),
            pltpu.VMEM((rows, LANES), f32),
            pltpu.VMEM((rows, LANES), f32),
            pltpu.VMEM((3, modes, SUB, LANES), f32),
        ],
        compiler_params=params,
        name="local_states",
    )(queries, keys_in, values_in, out_grad, before, after[:3], short_taps, pole_rate, residue)
    state_in, late_in = carried(final, first, rates, rows)
    query_grad, key_grad, value_grad, taps_sum, mode_sum, pole_sum = pl.pallas_call(
        functools.partial(second_kernel, members),
        grid=(chans // width,),
        in_specs=streams + [
            cut(3, SUB), cut(SUB), cut(3, tap_count), cut(3, wide_rows), cut(modes, SUB), cut(modes, SUB)
        ] + [cut(modes)] * 5,
        out_specs=[cut(rows)] * 3 + [cut(3, SUB), full(modes, local_groups), full(modes, local_groups)],
        out_shape=[arr(rows, chans, dtype=jnp.bfloat16)] * 3
        + [arr(3, SUB, chans), arr(modes, local_groups), arr(modes, local_groups)],
        scratch_shapes=[pltpu.VMEM((3, wide_rows, width), f32)]
        + [pltpu.VMEM((wide_rows, LANES), f32)] * 4
        + [pltpu.VMEM((3, wide_rows, width), f32)]
        + [pltpu.VMEM((modes, width), f32)] * 2
        + [pltpu.VMEM((6, modes, SUB, LANES), f32)]
        + [pltpu.VMEM((2, rows // SUB, SUB, LANES), f32)] * 2
        + [pltpu.VMEM((TOGETHER, rows // SUB, SUB, LANES), f32)],
        compiler_params=params,
        name="gradients",
    )(queries, keys_in, values_in, out_grad, before, after[3], short_taps, mix, ef, ea,
      final, rates, ress, state_in, late_in)
    taps_sum, mode_sum, pole_sum = summed_all(taps_sum, mode_sum, pole_sum)
    tap_grad = taps_sum[:, :tap_count] / jnp.sqrt(f32(token_total))
    return (query_grad, key_grad, value_grad, tap_grad, -pole_sum / f32(token_total), mode_sum / f32(token_total))


def summed_all(taps_sum, mode_sum, pole_sum):
    modes, groups = mode_sum.shape
    blocks = [taps_sum] + [x.reshape(modes // SUB, SUB, groups) for x in (mode_sum, pole_sum)]
    parts = [tiles(x) for x in blocks]
    total = summed(jnp.concatenate(parts, axis=0))
    results, start = [], 0
    for part, block in zip(parts, blocks):
        results.append(untiled(total[start:start + part.shape[0]], *block.shape))
        start += part.shape[0]
    return results[0], results[1].reshape(modes, groups), results[2].reshape(modes, groups)


def solution(mesh):
    tokens = P(("groups", "ctx", "inner"), "chan")
    return jax.shard_map(
        on_device,
        mesh=mesh,
        in_specs=(tokens, tokens, tokens, tokens, P(None, None, "chan"), P(None, "chan"), P(None, "chan")),
        out_specs=(
            tokens,
            tokens,
            tokens,
            P("groups", None, "chan"),
            P("groups", "chan"),
            P("groups", "chan"),
        ),
        check_vma=False,
    )
```

```python
import functools

import jax
import jax.numpy as jnp
from jax import lax
from jax.experimental import pallas as pl
from jax.experimental.pallas import tpu as pltpu
from jax.sharding import PartitionSpec as P

LINE = ("ctx", "inner")
LANES = 128
SUB = 8
TOGETHER = 8
PIECE = 512
MESH = pl.DeviceIdType.MESH


def moved(block, distance):
    devices = range(lax.axis_size(LINE))
    return lax.ppermute(block, LINE, [(i, i + distance) for i in devices if i + distance in devices])


def place_of(position):
    inner = lax.axis_size("inner")
    return {"ctx": position // inner, "inner": position % inner}


def carry_kernel(pieces, rows, final_ref, first_ref, rates_ref, sin_ref, pin_ref, near, outward, entering,
                 near_send, near_recv, far_send, far_recv, give_send, give_recv):
    inner, outer = lax.axis_size("inner"), lax.axis_size("ctx")
    x, z = lax.axis_index("inner"), lax.axis_index("ctx")
    width = final_ref.shape[1] // pieces
    barrier = pltpu.get_barrier_semaphore()
    others = [lax.rem(x + d, inner) for d in range(1, inner)]
    for other in others:
        pl.semaphore_signal(barrier, inc=1, device_id={"inner": other}, device_id_type=MESH)

    @pl.when(z > 0)
    def _():
        pl.semaphore_signal(barrier, inc=1, device_id={"ctx": z - 1}, device_id_type=MESH)

    @pl.when(z < outer - 1)
    def _():
        pl.semaphore_signal(barrier, inc=1, device_id={"ctx": z + 1}, device_id_type=MESH)

    pl.semaphore_wait(barrier, inner - 1 + jnp.where(z > 0, 1, 0) + jnp.where(z < outer - 1, 1, 0))

    def copy(source, target, send, recv, where):
        return pltpu.make_async_remote_copy(
            src_ref=source, dst_ref=target, send_sem=send, recv_sem=recv, device_id=where, device_id_type=MESH
        )

    lines = []
    for line, total_ref, into_ref in ((0, final_ref, sin_ref), (1, first_ref, pin_ref)):
        xs, zs = (x, z) if line == 0 else (inner - 1 - x, outer - 1 - z)
        lines.append((line, total_ref, into_ref, xs, zs, 1 if line == 0 else -1))

    def near_copy(line, total_ref, piece, steps, sign):
        cols = pl.ds(piece * width, width)
        return copy(
            total_ref.at[:, cols], near.at[line, steps - 1, :, cols],
            near_send.at[line, steps - 1, piece], near_recv.at[line, steps - 1, piece],
            {"inner": lax.rem(x + sign * steps + inner, inner)},
        )

    def far_copy(line, piece, sign):
        cols = pl.ds(piece * width, width)
        return copy(
            outward.at[line, :, cols], entering.at[line, :, cols],
            far_send.at[line, piece], far_recv.at[line, piece],
            {"ctx": lax.rem(z + sign + outer, outer)},
        )

    def give_copy(line, piece, steps, sign):
        cols = pl.ds(piece * width, width)
        return copy(
            entering.at[line, :, cols], entering.at[line, :, cols],
            give_send.at[line, steps - 1, piece], give_recv.at[line, piece],
            {"inner": lax.rem(x - sign * steps + inner, inner)},
        )

    for piece in range(pieces):
        for line, total_ref, _, xs, _, sign in lines:
            for steps in range(1, inner):
                @pl.when(xs + steps < inner)
                def _():
                    near_copy(line, total_ref, piece, steps, sign).start()

    for piece in range(pieces):
        cols = pl.ds(piece * width, width)
        decay = jnp.exp(rates_ref[:, cols] * -float(rows))
        for line, total_ref, into_ref, xs, zs, sign in lines:
            @pl.when(xs == inner - 1)
            def _():
                total = jnp.zeros_like(into_ref[:, cols])
                for steps in range(inner - 1, 0, -1):
                    near_copy(line, total_ref, piece, steps, sign).wait_recv()
                    total = decay * total + near[line, steps - 1, :, cols]
                into_ref[:, cols] = total

                @pl.when(zs == 0)
                def _():
                    entering[line, :, cols] = jnp.zeros_like(total)

                @pl.when(zs > 0)
                def _():
                    far_copy(line, piece, sign).wait_recv()

                power = jnp.exp(rates_ref[:, cols] * -float(rows * (inner - 1)))
                mine = power * entering[line, :, cols] + into_ref[:, cols]
                into_ref[:, cols] = mine

                @pl.when(zs < outer - 1)
                def _():
                    outward[line, :, cols] = decay * mine + total_ref[:, cols]
                    far_copy(line, piece, sign).start()

                for steps in range(1, inner):
                    give_copy(line, piece, steps, sign).start()

    for piece in range(pieces):
        cols = pl.ds(piece * width, width)
        decay = jnp.exp(rates_ref[:, cols] * -float(rows))
        for line, total_ref, into_ref, xs, zs, sign in lines:
            @pl.when(xs < inner - 1)
            def _():
                into_ref[:, cols] = jnp.zeros_like(into_ref[:, cols])
                for steps in range(inner - 2, 0, -1):
                    @pl.when(xs >= steps)
                    def _():
                        near_copy(line, total_ref, piece, steps, sign).wait_recv()
                        into_ref[:, cols] = decay * into_ref[:, cols] + near[line, steps - 1, :, cols]

                give_copy(line, piece, 1, sign).wait_recv()
                power = jnp.exp(rates_ref[:, cols] * (-float(rows) * xs.astype(jnp.float32)))
                into_ref[:, cols] = power * entering[line, :, cols] + into_ref[:, cols]

    for piece in range(pieces):
        for line, total_ref, _, xs, zs, sign in lines:
            for steps in range(1, inner):
                @pl.when(xs + steps < inner)
                def _():
                    near_copy(line, total_ref, piece, steps, sign).wait_send()

                @pl.when(xs == inner - 1)
                def _():
                    give_copy(line, piece, steps, sign).wait_send()

            @pl.when((xs == inner - 1) & (zs < outer - 1))
            def _():
                far_copy(line, piece, sign).wait_send()


def carried(final, first, rates, rows):
    modes, chans = final.shape
    pieces = max(1, chans // PIECE)
    hops = max(1, lax.axis_size("inner") - 1)
    shape = jax.ShapeDtypeStruct((modes, chans), jnp.float32)
    vmem = pl.BlockSpec(memory_space=pltpu.VMEM)
    return pl.pallas_call(
        functools.partial(carry_kernel, pieces, rows),
        in_specs=[vmem] * 3,
        out_specs=[vmem] * 2,
        out_shape=[shape] * 2,
        scratch_shapes=[
            pltpu.VMEM((2, hops, modes, chans), jnp.float32),
            pltpu.VMEM((2, modes, chans), jnp.float32),
            pltpu.VMEM((2, modes, chans), jnp.float32),
            pltpu.SemaphoreType.DMA((2, hops, pieces)),
            pltpu.SemaphoreType.DMA((2, hops, pieces)),
            pltpu.SemaphoreType.DMA((2, pieces)),
            pltpu.SemaphoreType.DMA((2, pieces)),
            pltpu.SemaphoreType.DMA((2, hops, pieces)),
            pltpu.SemaphoreType.DMA((2, pieces)),
        ],
        compiler_params=pltpu.CompilerParams(
            collective_id=0, has_side_effects=True, vmem_limit_bytes=16 * 1024 * 1024
        ),
        name="carry",
    )(final, first, rates)


def sum_kernel(x_ref, out_ref, land, send_sem, recv_sem):
    count = lax.axis_size(LINE)
    me = lax.axis_index("ctx") * lax.axis_size("inner") + lax.axis_index("inner")
    barrier = pltpu.get_barrier_semaphore()
    others = [lax.rem(me + d, count) for d in range(1, count)]
    for other in others:
        pl.semaphore_signal(barrier, inc=1, device_id=place_of(other), device_id_type=MESH)
    pl.semaphore_wait(barrier, count - 1)

    def copy_of(source, target, phase, d):
        return pltpu.make_async_remote_copy(
            src_ref=source,
            dst_ref=target,
            send_sem=send_sem.at[phase, d],
            recv_sem=recv_sem.at[phase, d],
            device_id=place_of(others[d]),
            device_id_type=MESH,
        )

    copies = [copy_of(x_ref.at[other], land.at[d], 0, d) for d, other in enumerate(others)]
    for copy in copies:
        copy.start()
    total = x_ref[me]
    for d, copy in enumerate(copies):
        copy.wait_recv()
        total = total + land[d]
    out_ref[me] = total
    spreads = [copy_of(out_ref.at[me], out_ref.at[me], 1, d) for d in range(count - 1)]
    for copy in spreads:
        copy.start()
    for copy in copies:
        copy.wait_send()
    for d in range(count - 1):
        source = lax.rem(me + count - 1 - d, count)
        copy_of(out_ref.at[me], out_ref.at[source], 1, d).wait_recv()
    for copy in spreads:
        copy.wait_send()


def summed(block):
    count = lax.axis_size(LINE)
    rows = block.shape[0]
    each = -(-rows // (count * SUB)) * SUB
    padded = jnp.pad(block, ((0, each * count - rows), (0, 0))).reshape(count, each, LANES)
    vmem = pl.BlockSpec(memory_space=pltpu.VMEM)
    result = pl.pallas_call(
        sum_kernel,
        in_specs=[vmem],
        out_specs=vmem,
        out_shape=jax.ShapeDtypeStruct(padded.shape, jnp.float32),
        scratch_shapes=[
            pltpu.VMEM((count - 1, each, LANES), jnp.float32),
            pltpu.SemaphoreType.DMA((2, count - 1)),
            pltpu.SemaphoreType.DMA((2, count - 1)),
        ],
        compiler_params=pltpu.CompilerParams(
            collective_id=1, has_side_effects=True, vmem_limit_bytes=16 * 1024 * 1024
        ),
        name="sums",
    )(padded)
    return result.reshape(count * each, LANES)[:rows]


def tiles(block):
    lead, sub, chans = block.shape
    return block.reshape(lead, sub, chans // LANES, LANES).transpose(0, 2, 1, 3).reshape(-1, LANES)


def untiled(flat, lead, sub, chans):
    return flat.reshape(lead, chans // LANES, sub, LANES).transpose(0, 2, 1, 3).reshape(lead, sub, chans)


def spread_matrix(local_groups, width, members, over_rows):
    shape = (width, local_groups) if over_rows else (local_groups, width)
    chan = lax.broadcasted_iota(jnp.int32, shape, 0 if over_rows else 1) + pl.program_id(0) * width
    low = lax.broadcasted_iota(jnp.int32, shape, 1 if over_rows else 0) * members
    return jnp.where((chan >= low) & (chan < low + members), 1.0, 0.0).astype(jnp.bfloat16)


def table_dots(tables, onto):
    terms = []
    for rest in tables:
        for _ in range(3):
            term = rest.astype(jnp.bfloat16)
            terms.append(term)
            rest = rest - term.astype(jnp.float32)
    rows = tables[0].shape[0]
    out = jnp.dot(jnp.concatenate(terms, axis=0), onto, preferred_element_type=jnp.float32)
    cut = [out[i * rows:(i + 1) * rows] for i in range(len(terms))]
    return [cut[3 * i] + cut[3 * i + 1] + cut[3 * i + 2] for i in range(len(tables))]


def first_kernel(members, q_ref, k_ref, v_ref, g_ref, prev_ref, next_ref, taps_ref, rate_ref, res_ref,
                 mix_ref, ef_ref, ea_ref, final_ref, first_ref, rates_ref, ress_ref, wide, src, adj, each):
    rows, width = q_ref.shape
    modes, local_groups = rate_ref.shape
    tap_count = taps_ref.shape[1]
    steps = rows // SUB
    onto = spread_matrix(local_groups, width, members, False)
    rates_ref[...], ress_ref[...] = table_dots([rate_ref[...], res_ref[...]], onto)
    for i, x_ref in enumerate((q_ref, k_ref, v_ref)):
        wide[i, 0:SUB] = prev_ref[i]
        wide[i, SUB:SUB + rows] = x_ref[...].astype(jnp.float32)
        wide[i, SUB + rows:] = next_ref[i]
    chunk = lax.broadcasted_iota(jnp.int32, (SUB, LANES), 0).astype(jnp.float32)

    @pl.loop(0, width // LANES)
    def _(column):
        cols = pl.ds(pl.multiple_of(column * LANES, LANES), LANES)
        mixes = []
        for i in range(3):
            total = taps_ref[i, 0:1, cols] * wide[i, SUB:, cols]
            for j in range(1, tap_count):
                total = total + taps_ref[i, j:j + 1, cols] * wide[i, SUB - j:2 * SUB + rows - j, cols]
            mix_ref[i, :, cols] = total
            mixes.append(total[:rows])
        src[:, :] = mixes[1] * mixes[2]
        adj[:, :] = mixes[0] * g_ref[:, cols].astype(jnp.float32)
        s = [src[pl.ds(j, SUB, stride=steps), :] for j in range(steps)]
        a = [adj[pl.ds(j, SUB, stride=steps), :] for j in range(steps)]

        for n in range(modes):
            each[0, n] = jnp.broadcast_to(rates_ref[n:n + 1, cols], (SUB, LANES))

        def one(n, nothing):
            rate = each[0, n]
            lam = jnp.exp(-rate)
            ahead = s[0]
            back = a[steps - 1]
            for j in range(1, steps):
                ahead = lam * ahead + s[j]
                back = lam * back + a[steps - 1 - j]
            ef_ref[n, :, cols] = ahead
            ea_ref[n, :, cols] = back
            later = jnp.exp(rate * ((chunk - (SUB - 1)) * float(steps)))
            sooner = jnp.exp(rate * (chunk * -float(steps)))
            each[1, n] = ahead * later
            each[2, n] = back * sooner
            return nothing

        lax.fori_loop(0, modes, one, 0, unroll=4)
        final_ref[:, cols] = jnp.sum(each[1], axis=1)
        first_ref[:, cols] = jnp.sum(each[2], axis=1)


def second_kernel(members, q_ref, k_ref, v_ref, g_ref, prev_ref, gnext_ref, taps_ref, mix_ref, ef_ref, ea_ref,
                  final_ref, rates_ref, ress_ref, sin_ref, pin_ref,
                  qg_ref, kg_ref, vg_ref, tap_ref, mode_ref, pole_ref,
                  wide, src, adj, long_out, long_adj, back, mode_rows, pole_rows, each, sums, terms, held):
    rows, width = q_ref.shape
    modes = rates_ref.shape[0]
    local_groups = mode_ref.shape[1]
    tap_count = taps_ref.shape[1]
    steps = rows // SUB
    for i, x_ref in enumerate((q_ref, k_ref, v_ref)):
        wide[i, 0:SUB] = prev_ref[i]
        wide[i, SUB:] = x_ref[...].astype(jnp.float32)
    chunk = lax.broadcasted_iota(jnp.int32, (SUB, LANES), 0)

    @pl.loop(0, width // LANES)
    def _(column):
        cols = pl.ds(pl.multiple_of(column * LANES, LANES), LANES)
        src[:, :] = mix_ref[1, :, cols] * mix_ref[2, :, cols]
        adj[:rows, :] = mix_ref[0, :rows, cols] * g_ref[:, cols].astype(jnp.float32)
        adj[rows:, :] = mix_ref[0, rows:, cols] * gnext_ref[:, cols]
        s = [src[pl.ds(j, SUB, stride=steps), :] for j in range(steps)]
        a = [adj[pl.ds(j, SUB, stride=steps), :] for j in range(steps)]
        zero = jnp.zeros((SUB, LANES), jnp.float32)

        lam_table = jnp.exp(-rates_ref[:, cols])
        decay_table = jnp.exp(rates_ref[:, cols] * -float(steps))
        for i, table in enumerate((lam_table, ress_ref[:, cols])):
            for n in range(modes):
                each[i, n] = jnp.broadcast_to(table[n:n + 1], (SUB, LANES))
        for n in range(modes):
            decay = jnp.broadcast_to(decay_table[n:n + 1], (SUB, LANES))
            state = jnp.where(chunk == 0, sin_ref[n:n + 1, cols], pltpu.roll(ef_ref[n, :, cols], 1, 0))
            late = jnp.where(
                chunk == SUB - 1, pin_ref[n:n + 1, cols], pltpu.roll(ea_ref[n, :, cols], SUB - 1, 0)
            )
            distance = 1
            while distance < SUB:
                state = state + jnp.where(chunk >= distance, decay * pltpu.roll(state, distance, 0), 0.0)
                late = late + jnp.where(chunk < SUB - distance, decay * pltpu.roll(late, SUB - distance, 0), 0.0)
                decay = decay * decay
                distance *= 2
            each[2, n] = state
            each[3, n] = late
        for j in range(steps):
            sums[0, j] = zero
            sums[1, j] = zero
            terms[0, j] = s[j]
            terms[1, j] = a[j]

        @pl.loop(0, modes // TOGETHER)
        def _(group):
            here = [group * TOGETHER + m for m in range(TOGETHER)]
            lam = [each[0, n] for n in here]
            res = [each[1, n] for n in here]
            state = [each[2, n] for n in here]
            late = [each[3, n] for n in here]
            mode_sum = [zero] * TOGETHER
            pole_sum = [zero] * TOGETHER
            for j in range(steps):
                source, toward, out = terms[0, j], terms[1, j], sums[0, j]
                for m in range(TOGETHER):
                    held[m, j] = state[m]
                    state[m] = lam[m] * state[m] + source
                    out = out + res[m] * state[m]
                    mode_sum[m] = mode_sum[m] + toward * state[m]
                sums[0, j] = out
            for j in range(steps - 1, -1, -1):
                toward, out = terms[1, j], sums[1, j]
                for m in range(TOGETHER):
                    late[m] = lam[m] * late[m] + toward
                    out = out + res[m] * late[m]
                    pole_sum[m] = pole_sum[m] + late[m] * held[m, j]
                sums[1, j] = out
            for m, n in enumerate(here):
                each[4, n] = mode_sum[m]
                each[5, n] = lam[m] * res[m] * pole_sum[m]

        mode_rows[:, cols] = jnp.sum(each[4], axis=1)
        pole_rows[:, cols] = jnp.sum(each[5], axis=1)
        for j in range(steps):
            long_out[pl.ds(j, SUB, stride=steps), :] = sums[0, j]
            long_adj[pl.ds(j, SUB, stride=steps), :] = sums[1, j]
        rate = rates_ref[:, cols]
        res = ress_ref[:, cols]
        lam = jnp.exp(-rate)
        grow = jnp.exp(rate)
        state = jnp.exp(rate * -float(rows)) * sin_ref[:, cols] + final_ref[:, cols]
        late = pin_ref[:, cols]
        long_out[rows:, :] = zero
        long_adj[rows:, :] = zero
        for j in range(tap_count - 1):
            state = lam * state + src[rows + j:rows + j + 1, :]
            long_out[rows + j:rows + j + 1, :] = jnp.sum(res * state, axis=0, keepdims=True)
            long_adj[rows + j:rows + j + 1, :] = jnp.sum(res * late, axis=0, keepdims=True)
            late = (late - adj[rows + j:rows + j + 1, :]) * grow
        back[0, :rows, cols] = g_ref[:, cols].astype(jnp.float32) * long_out[:rows, :]
        back[0, rows:, cols] = gnext_ref[:, cols] * long_out[rows:, :]
        back[1, :, cols] = long_adj[:, :] * mix_ref[2, :, cols]
        back[2, :, cols] = long_adj[:, :] * mix_ref[1, :, cols]
        for i, grad_ref in enumerate((qg_ref, kg_ref, vg_ref)):
            mine = back[i, 0:rows, cols]
            total = taps_ref[i, 0:1, cols] * mine
            for j in range(1, tap_count):
                total = total + taps_ref[i, j:j + 1, cols] * back[i, j:j + rows, cols]
            grad_ref[:, cols] = total.astype(grad_ref.dtype)
            for j in range(tap_count):
                tap_ref[i, j:j + 1, cols] = jnp.sum(
                    mine * wide[i, SUB - j:SUB - j + rows, cols], axis=0, keepdims=True
                )
            for j in range(tap_count, SUB):
                tap_ref[i, j:j + 1, cols] = jnp.zeros((1, LANES), jnp.float32)

    onto = spread_matrix(local_groups, width, members, True)
    mode_part, pole_part = table_dots([mode_rows[...], pole_rows[...]], onto)

    @pl.when(pl.program_id(0) == 0)
    def _():
        mode_ref[...] = jnp.zeros_like(mode_ref)
        pole_ref[...] = jnp.zeros_like(pole_ref)

    mode_ref[...] += mode_part
    pole_ref[...] += pole_part


def on_device(queries, keys_in, values_in, out_grad, short_taps, pole_rate, residue):
    rows, chans = queries.shape
    modes, local_groups = pole_rate.shape
    members = chans // local_groups
    tap_count = short_taps.shape[1]
    token_total = rows * lax.axis_size(LINE)
    width = min(512, chans)
    f32 = jnp.float32
    tails = jnp.stack([x[rows - SUB:] for x in (queries, keys_in, values_in)])
    heads = jnp.stack([x[:SUB] for x in (queries, keys_in, values_in, out_grad)])
    before = moved(tails, 1).astype(f32)
    after = moved(heads, -1).astype(f32)

    def cut(*lead):
        zeros = (0,) * len(lead)
        return pl.BlockSpec((*lead, width), lambda i: (*zeros, i))

    def full(*shape):
        zeros = (0,) * len(shape)
        return pl.BlockSpec(shape, lambda i: zeros)

    def arr(*shape, dtype=f32):
        return jax.ShapeDtypeStruct(shape, dtype)

    params = pltpu.CompilerParams(vmem_limit_bytes=48 * 1024 * 1024)
    wide_rows = rows + SUB
    streams = [cut(rows)] * 4
    mix, ef, ea, final, first, rates, ress = pl.pallas_call(
        functools.partial(first_kernel, members),
        grid=(chans // width,),
        in_specs=streams + [
            cut(3, SUB), cut(3, SUB), cut(3, tap_count), full(modes, local_groups), full(modes, local_groups)
        ],
        out_specs=[cut(3, wide_rows), cut(modes, SUB), cut(modes, SUB)] + [cut(modes)] * 4,
        out_shape=[arr(3, wide_rows, chans), arr(modes, SUB, chans), arr(modes, SUB, chans)]
        + [arr(modes, chans)] * 4,
        scratch_shapes=[
            pltpu.VMEM((3, wide_rows + SUB, width), f32),
            pltpu.VMEM((rows, LANES), f32),
            pltpu.VMEM((rows, LANES), f32),
            pltpu.VMEM((3, modes, SUB, LANES), f32),
        ],
        compiler_params=params,
        name="local_states",
    )(queries, keys_in, values_in, out_grad, before, after[:3], short_taps, pole_rate, residue)
    state_in, late_in = carried(final, first, rates, rows)
    query_grad, key_grad, value_grad, taps_sum, mode_sum, pole_sum = pl.pallas_call(
        functools.partial(second_kernel, members),
        grid=(chans // width,),
        in_specs=streams + [
            cut(3, SUB), cut(SUB), cut(3, tap_count), cut(3, wide_rows), cut(modes, SUB), cut(modes, SUB)
        ] + [cut(modes)] * 5,
        out_specs=[cut(rows)] * 3 + [cut(3, SUB), full(modes, local_groups), full(modes, local_groups)],
        out_shape=[arr(rows, chans, dtype=jnp.bfloat16)] * 3
        + [arr(3, SUB, chans), arr(modes, local_groups), arr(modes, local_groups)],
        scratch_shapes=[pltpu.VMEM((3, wide_rows, width), f32)]
        + [pltpu.VMEM((wide_rows, LANES), f32)] * 4
        + [pltpu.VMEM((3, wide_rows, width), f32)]
        + [pltpu.VMEM((modes, width), f32)] * 2
        + [pltpu.VMEM((6, modes, SUB, LANES), f32)]
        + [pltpu.VMEM((2, rows // SUB, SUB, LANES), f32)] * 2
        + [pltpu.VMEM((TOGETHER, rows // SUB, SUB, LANES), f32)],
        compiler_params=params,
        name="gradients",
    )(queries, keys_in, values_in, out_grad, before, after[3], short_taps, mix, ef, ea,
      final, rates, ress, state_in, late_in)
    taps_sum, mode_sum, pole_sum = summed_all(taps_sum, mode_sum, pole_sum)
    tap_grad = taps_sum[:, :tap_count] / jnp.sqrt(f32(token_total))
    return (query_grad, key_grad, value_grad, tap_grad, -pole_sum / f32(token_total), mode_sum / f32(token_total))


def summed_all(taps_sum, mode_sum, pole_sum):
    modes, groups = mode_sum.shape
    blocks = [taps_sum] + [x.reshape(modes // SUB, SUB, groups) for x in (mode_sum, pole_sum)]
    parts = [tiles(x) for x in blocks]
    total = summed(jnp.concatenate(parts, axis=0))
    results, start = [], 0
    for part, block in zip(parts, blocks):
        results.append(untiled(total[start:start + part.shape[0]], *block.shape))
        start += part.shape[0]
    return results[0], results[1].reshape(modes, groups), results[2].reshape(modes, groups)


def solution(mesh):
    tokens = P(("groups", "ctx", "inner"), "chan")
    return jax.shard_map(
        on_device,
        mesh=mesh,
        in_specs=(tokens, tokens, tokens, tokens, P(None, None, "chan"), P(None, "chan"), P(None, "chan")),
        out_specs=(
            tokens,
            tokens,
            tokens,
            P("groups", None, "chan"),
            P("groups", "chan"),
            P("groups", "chan"),
        ),
        check_vma=False,
    )
```
